32 devices in a mesh: dp: 8 (over z, x), tensor: 4 (over y, core).
Axes of the slice: x: 2, y: 2, z: 4, core: 2. Of those that a mesh axis runs over, the one named last changes fastest.
Arguments:
- encoder_rows: bfloat16 [8192, 768], P(('dp', 'tensor')), may hold values from -6 to 6
- decoder_rows: bfloat16 [4096, 768], P(('dp', 'tensor')), may hold values from -6 to 6
- encoder_segments: int32 [8, 1024], P('dp'), may hold values from 0 to 3, as said below
- decoder_segments: int32 [8, 512], P('dp'), may hold values from 0 to 3, as said below
- norm_gains: float32 [6, 768], replicated, may hold values from 0.5 to 1.5
- encoder_attention_in: bfloat16 [768, 3, 768], P(None, None, 'tensor'), may hold values from -0.109375 to 0.109375
- encoder_attention_out: bfloat16 [768, 768], P('tensor'), may hold values from -1.75 to 1.75
- encoder_gate_up: bfloat16 [768, 2, 2048], P(None, None, 'tensor'), may hold values from -0.21875 to 0.21875
- encoder_down: bfloat16 [2048, 768], P('tensor'), may hold values from -0.1875 to 0.1875
- decoder_attention_in: bfloat16 [768, 3, 768], P(None, None, 'tensor'), may hold values from -0.109375 to 0.109375
- decoder_attention_out: bfloat16 [768, 768], P('tensor'), may hold values from -1.75 to 1.75
- cross_queries: bfloat16 [768, 768], P(None, 'tensor'), may hold values from -0.109375 to 0.109375
- cross_key_value_rows: bfloat16 [768, 2, 768], P(None, None, 'tensor'), may hold values from -0.109375 to 0.109375
- cross_output: bfloat16 [768, 768], P('tensor'), may hold values from -1.75 to 1.75
- decoder_gate_up: bfloat16 [768, 2, 2048], P(None, None, 'tensor'), may hold values from -0.21875 to 0.21875
- decoder_down: bfloat16 [2048, 768], P('tensor'), may hold values from -0.1875 to 0.1875
- position_tables: float32 [2, 32, 12], P(None, None, 'tensor'), may hold values from -6 to 6
- encoder_cotangent: bfloat16 [8192, 768], P(('dp', 'tensor')), may hold values from -6 to 6
- decoder_cotangent: bfloat16 [4096, 768], P(('dp', 'tensor')), may hold values from -6 to 6
Outputs:
- encoder_result: bfloat16 [8192, 768], P(('dp', 'tensor'))
- decoder_result: bfloat16 [4096, 768], P(('dp', 'tensor'))
- encoder_rows_gradient: float32 [8192, 768], P(('dp', 'tensor'))
- decoder_rows_gradient: float32 [4096, 768], P(('dp', 'tensor'))
- norm_gains_gradient: float32 [6, 768], replicated
- encoder_attention_in_gradient: float32 [768, 3, 768], P(None, None, 'tensor')
- encoder_attention_out_gradient: float32 [768, 768], P('tensor')
- encoder_gate_up_gradient: float32 [768, 2, 2048], P(None, None, 'tensor')
- encoder_down_gradient: float32 [2048, 768], P('tensor')
- decoder_attention_in_gradient: float32 [768, 3, 768], P(None, None, 'tensor')
- decoder_attention_out_gradient: float32 [768, 768], P('tensor')
- cross_queries_gradient: float32 [768, 768], P(None, 'tensor')
- cross_keys_values_gradient: float32 [768, 2, 768], P(None, None, 'tensor')
- cross_output_gradient: float32 [768, 768], P('tensor')
- decoder_gate_up_gradient: float32 [768, 2, 2048], P(None, None, 'tensor')
- decoder_down_gradient: float32 [2048, 768], P('tensor')
- position_tables_gradient: float32 [2, 32, 12], P(None, None, 'tensor')
The draws below stay inside these ranges and needn't reach their ends.
Inputs may be any that keep to these rules, and one draw needn't show every extreme that they name: `encoder_segments`: each row holds 4 segments numbered 0 to 3 in order, each of 2 or more positions. `decoder_segments`: each row holds 4 segments numbered 0 to 3 in order, each of 2 or more positions; segment k of a decoder row belongs to segment k of the same encoder row.
All inputs are finite; a program needn't handle non-finite values.
Results may differ from the reference program's by a relative error of at most 0.025.
The reference program's roundings to bfloat16 on the way count: a program that leaves them out, or rounds other values in their place, can miss the bound.
Values may be sent and summed in bfloat16 or wider, within the bound.
A program may use at most 512 MiB of HBM per device.

```python
import math
import jax
import jax.numpy as jnp
from jax import lax

D = 768
HEAD_COUNT = 12
HEAD_FEATURES = 64
FF = 2048
BUCKETS = 32
ENCODER_LENGTH = 1024
DEC_LEN = 512
SEGS = 4
INNER = 768
SEQS = 8
ENC_ROWS = 8192
DEC_ROWS = 4096


def segment_ids(key, row_count, length):
    stride = length // SEGS
    jitter = stride // 2 - 1
    offsets = jax.random.randint(key, (row_count, SEGS - 1), -jitter, jitter + 1)
    boundaries = jnp.arange(1, SEGS, dtype=jnp.int32)[None, :] * stride + offsets
    positions = jnp.arange(length, dtype=jnp.int32)
    return jnp.sum((positions[None, :, None] >= boundaries[:, None, :]).astype(jnp.int32), axis=-1).astype(jnp.int32)


def draw_encoder_segments(key, part):
    return segment_ids(jax.random.fold_in(key, 11), SEQS, ENCODER_LENGTH)


def draw_decoder_segments(key, part):
    return segment_ids(jax.random.fold_in(key, 23), SEQS, DEC_LEN)


def shard_levels(own_key, shape, pieces, low, high):
    loudness, own = 1.0, jax.random.fold_in(own_key, 6)
    for dim, blocks in pieces:
        steps = jnp.exp(jax.random.uniform(jax.random.fold_in(own, dim), (blocks,), jnp.float32, low / len(pieces), high / len(pieces)))
        loudness = loudness * jnp.repeat(steps, shape[dim] // blocks).reshape([-1 if axis == dim else 1 for axis in range(len(shape))])
    return loudness


def centred(rng, dims, spread, bound, pieces=(), held_as=jnp.bfloat16):
    entries = spread * jax.random.normal(rng, dims, jnp.float32)
    if pieces:
        entries = entries * shard_levels(rng, dims, pieces, -0.22, 0.18)
    return jnp.clip(entries, -bound, bound).astype(held_as)


def setup_inputs(seed: int = 0) -> dict:
    key_of = jax.random.split(jax.random.key(seed), 20)
    return {
        "encoder_rows": centred(key_of[0], (ENC_ROWS, D), 1.0, 6.0, ((0, 32),)),
        "decoder_rows": centred(key_of[1], (DEC_ROWS, D), 1.0, 6.0, ((0, 32),)),
        "encoder_segments": draw_encoder_segments(jax.random.fold_in(key_of[19], 71), 0),
        "decoder_segments": draw_decoder_segments(jax.random.fold_in(key_of[19], 71), 0),
        "norm_gains": jnp.clip(1.0 + 0.1 * jax.random.normal(key_of[4], (6, D), jnp.float32), 0.5, 1.5),
        "encoder_attention_in": centred(key_of[5], (D, 3, INNER), (0.5 * D ** -0.5), 0.109375, ((2, 4),)),
        "encoder_attention_out": centred(key_of[6], (INNER, D), (8.0 * INNER ** -0.5), 1.75, ((0, 4),)),
        "encoder_gate_up": centred(key_of[7], (D, 2, FF), D ** -0.5, 0.21875, ((2, 4),)),
        "encoder_down": centred(key_of[8], (FF, D), (1.5 * FF ** -0.5), 0.1875, ((0, 4),)),
        "decoder_attention_in": centred(key_of[9], (D, 3, INNER), (0.5 * D ** -0.5), 0.109375, ((2, 4),)),
        "decoder_attention_out": centred(key_of[10], (INNER, D), (8.0 * INNER ** -0.5), 1.75, ((0, 4),)),
        "cross_queries": centred(key_of[11], (D, INNER), (0.5 * D ** -0.5), 0.109375, ((1, 4),)),
        "cross_key_value_rows": centred(key_of[12], (D, 2, INNER), (0.5 * D ** -0.5), 0.109375, ((2, 4),)),
        "cross_output": centred(key_of[13], (INNER, D), (8.0 * INNER ** -0.5), 1.75, ((0, 4),)),
        "decoder_gate_up": centred(key_of[14], (D, 2, FF), D ** -0.5, 0.21875, ((2, 4),)),
        "decoder_down": centred(key_of[15], (FF, D), (1.5 * FF ** -0.5), 0.1875, ((0, 4),)),
        "position_tables": centred(key_of[16], (2, BUCKETS, HEAD_COUNT), 1.0, 6.0, ((2, 4),), jnp.float32),
        "encoder_cotangent": centred(key_of[17], (ENC_ROWS, D), 1.0, 6.0, ((0, 32),)),
        "decoder_cotangent": centred(key_of[18], (DEC_ROWS, D), 1.0, 6.0, ((0, 32),)),
    }


EPS = 1e-06
NEG = -1e+30

@jax.custom_vjp
def low(v):
    return lax.optimization_barrier(v.astype(jnp.bfloat16)).astype(jnp.float32)

@jax.custom_vjp
def low_back(v):
    return v

def low_keep(v):
    return (low(v), None)

def low_pass(kept, grad):
    return (grad,)

def back_keep(v):
    return (v, None)

def back_low(kept, grad):
    return (low(grad),)
low.defvjp(low_keep, low_pass)
low_back.defvjp(back_keep, back_low)

def bucket_limits(exact_range, far_range, bucket_count):
    limits = []
    for level_index in range(1, bucket_count - exact_range):
        candidate = exact_range
        while int(math.log(candidate / exact_range) / math.log(far_range / exact_range) * (bucket_count - exact_range)) < level_index:
            candidate += 1
        limits.append(candidate)
    return limits

def relative_buckets(offsets, both_sides):
    if both_sides:
        bucket_count = BUCKETS // 2
        direction_base = jnp.where(offsets > 0, bucket_count, 0).astype(jnp.int32)
        distance = jnp.abs(offsets)
    else:
        bucket_count = BUCKETS
        direction_base = jnp.zeros_like(offsets)
        distance = jnp.maximum(-offsets, 0)
    exact_range = bucket_count // 2
    far_bucket = jnp.full_like(distance, exact_range)
    for limit_value in bucket_limits(exact_range, 128, bucket_count):
        far_bucket = far_bucket + (distance >= limit_value).astype(jnp.int32)
    return direction_base + jnp.where(distance < exact_range, distance, far_bucket)

def rounded_pair(value):
    return low_back(low(value))

def normalize(residual, gain_row):
    scale_row = lax.rsqrt(lax.optimization_barrier(jnp.mean(residual * residual, axis=-1, keepdims=True)) + EPS)
    return residual * scale_row * gain_row

def block_output(block_items, key_rows, value_rows, key_segments, bias_table, attention_kind):
    query_block, segment_block, row_start = block_items
    block_rows = query_block.shape[0]
    scores = jnp.einsum('bhd,lhd->hbl', query_block, key_rows, precision=lax.Precision.HIGHEST)
    rows_here = row_start + jnp.arange(block_rows, dtype=jnp.int32)
    columns = jnp.arange(key_rows.shape[0], dtype=jnp.int32)
    allowed = segment_block[:, None] == key_segments[None, :]
    if attention_kind != 'cross':
        buckets = relative_buckets(columns[None, :] - rows_here[:, None], attention_kind == 'encoder')
        scores = scores + jnp.transpose(jnp.take(bias_table, buckets, axis=0), (2, 0, 1))
    if attention_kind == 'decoder':
        allowed = allowed & (columns[None, :] <= rows_here[:, None])
    scores = low_back(scores)
    masked = jnp.where(allowed[None], scores, NEG)
    row_peak = lax.optimization_barrier(jnp.max(masked, axis=-1, keepdims=True))
    exponent = jnp.exp(masked - row_peak)
    probabilities = low(exponent / lax.optimization_barrier(jnp.sum(exponent, axis=-1, keepdims=True)))
    return jnp.einsum('hbl,lhd->bhd', probabilities, value_rows, precision=lax.Precision.HIGHEST)
checkpointed_block = jax.checkpoint(block_output, static_argnums=(5,))

def attend(query_rows, key_rows, value_rows, query_segments, key_segments, bias_table, attention_kind):
    length = query_rows.shape[0]
    block_rows = min(512, length)
    block_count = length // block_rows
    query_blocks = query_rows.reshape(block_count, block_rows, HEAD_COUNT, HEAD_FEATURES)
    segment_blocks = query_segments.reshape(block_count, block_rows)
    starts = jnp.arange(block_count, dtype=jnp.int32) * block_rows

    def one_block(block_items):
        return checkpointed_block(block_items, key_rows, value_rows, key_segments, bias_table, attention_kind)
    return lax.map(one_block, (query_blocks, segment_blocks, starts)).reshape(length, HEAD_COUNT, HEAD_FEATURES)

def self_attention(normalized_rows, input_weight, weight_out, segments, bias_table, attention_kind):
    length = normalized_rows.shape[0]
    projected_rows = rounded_pair(jnp.einsum('sk,kym->sym', normalized_rows, input_weight, precision=lax.Precision.HIGHEST))
    split_rows = projected_rows.reshape(length, 3, HEAD_COUNT, HEAD_FEATURES)
    attended = attend(split_rows[:, 0], split_rows[:, 1], split_rows[:, 2], segments, segments, bias_table, attention_kind)
    attended = rounded_pair(attended.reshape(length, HEAD_COUNT * HEAD_FEATURES))
    return low_back(jnp.dot(attended, weight_out, precision=lax.Precision.HIGHEST))

def feed_forward(normalized_rows, gate_up_matrix, down_weight):
    gate_up_rows = jnp.einsum('sk,kym->sym', normalized_rows, gate_up_matrix, precision=lax.Precision.HIGHEST)
    hidden = low(jax.nn.gelu(low_back(gate_up_rows[:, 0])) * low_back(gate_up_rows[:, 1]))
    return low_back(jnp.dot(hidden, down_weight, precision=lax.Precision.HIGHEST))

def sequence_forward(weight_set, sequence_items):
    gain_set, attention_in_one, attention_out_one, gate_up_one, down_one, attention_in_two, attention_out_two, cross_query_weight, cross_key_value_weight, cross_output_weight, gate_up_two, down_two, tables = weight_set
    encoder_input, decoder_input, encoder_segments, decoder_segments = sequence_items
    attention_rows = low(normalize(encoder_input, gain_set[0]))
    encoder_middle = encoder_input + self_attention(attention_rows, attention_in_one, attention_out_one, encoder_segments, tables[0], 'encoder')
    feed_rows = low(normalize(encoder_middle, gain_set[1]))
    encoder_last = encoder_middle + feed_forward(feed_rows, gate_up_one, down_one)
    encoder_result = normalize(encoder_last, gain_set[2])
    closing_rows = low(encoder_result)
    self_rows = low(normalize(decoder_input, gain_set[3]))
    decoder_middle = decoder_input + self_attention(self_rows, attention_in_two, attention_out_two, decoder_segments, tables[1], 'decoder')
    cross_rows = low(normalize(decoder_middle, gain_set[4]))
    query_rows = rounded_pair(jnp.dot(cross_rows, cross_query_weight, precision=lax.Precision.HIGHEST)).reshape(DEC_LEN, HEAD_COUNT, HEAD_FEATURES)
    key_value_rows = rounded_pair(jnp.einsum('sk,kym->sym', closing_rows, cross_key_value_weight, precision=lax.Precision.HIGHEST)).reshape(ENCODER_LENGTH, 2, HEAD_COUNT, HEAD_FEATURES)
    attended = attend(query_rows, key_value_rows[:, 0], key_value_rows[:, 1], decoder_segments, encoder_segments, None, 'cross')
    attended = rounded_pair(attended.reshape(DEC_LEN, HEAD_COUNT * HEAD_FEATURES))
    decoder_later = decoder_middle + low_back(jnp.dot(attended, cross_output_weight, precision=lax.Precision.HIGHEST))
    last_rows = low(normalize(decoder_later, gain_set[5]))
    return (encoder_result, decoder_later + feed_forward(last_rows, gate_up_two, down_two))

def reference(encoder_rows, decoder_rows, encoder_segments, decoder_segments, norm_gains, encoder_attention_in, encoder_attention_out, encoder_gate_up, encoder_down, decoder_attention_in, decoder_attention_out, cross_queries, cross_key_value_rows, cross_output, decoder_gate_up, decoder_down, position_tables, encoder_cotangent, decoder_cotangent):
    weights = tuple((weight_item.astype(jnp.float32) for weight_item in (norm_gains, encoder_attention_in, encoder_attention_out, encoder_gate_up, encoder_down, decoder_attention_in, decoder_attention_out, cross_queries, cross_key_value_rows, cross_output, decoder_gate_up, decoder_down, position_tables)))
    encoder_input = encoder_rows.astype(jnp.float32).reshape(SEQS, ENCODER_LENGTH, D)
    decoder_input = decoder_rows.astype(jnp.float32).reshape(SEQS, DEC_LEN, D)
    sequence_step = jax.checkpoint(sequence_forward)

    def forward(encoder_stack, decoder_stack, weight_set):

        def scan_step(carried, sequence_items):
            return (carried, sequence_step(weight_set, sequence_items))
        carried, results = lax.scan(scan_step, jnp.zeros((), jnp.float32), (encoder_stack, decoder_stack, encoder_segments, decoder_segments))
        return results
    results, pullback = jax.vjp(forward, encoder_input, decoder_input, weights)
    cotangents = (encoder_cotangent.astype(jnp.float32).reshape(SEQS, ENCODER_LENGTH, D), decoder_cotangent.astype(jnp.float32).reshape(SEQS, DEC_LEN, D))
    encoder_grad, decoder_grad, weight_grads = pullback(cotangents)
    return (results[0].reshape(ENC_ROWS, D).astype(jnp.bfloat16), results[1].reshape(DEC_ROWS, D).astype(jnp.bfloat16), encoder_grad.reshape(ENC_ROWS, D), decoder_grad.reshape(DEC_ROWS, D), weight_grads[0], weight_grads[1], weight_grads[2], weight_grads[3], weight_grads[4], weight_grads[5], weight_grads[6], weight_grads[7], weight_grads[8], weight_grads[9], weight_grads[10], weight_grads[11], weight_grads[12])
```

```python
import functools, math
import jax
import jax.numpy as jnp
from jax import lax
from jax.experimental import pallas as pl
from jax.experimental.pallas import tpu as pltpu
from jax.sharding import PartitionSpec as P

BUCKETS = 32
EPS = 1e-06
NEG = -1e30
VMEM_BYTES = 56 * 2**20


def bucket_limits(exact_range, far_range, bucket_count):
    limits = []
    for level_index in range(1, bucket_count - exact_range):
        candidate = exact_range
        while (int(math.log(candidate / exact_range) / math.log(far_range / exact_range) * (bucket_count - exact_range)) < level_index):
            candidate += 1
        limits.append(candidate)
    return limits

def side_starts(count):
    exact = count // 2
    return list(range(exact + 1)) + bucket_limits(exact, 128, count)

def bucket_ranges(kind):
    far = 1 << 20
    if kind == "encoder":
        starts = side_starts(BUCKETS // 2)
        ends = [s - 1 for s in starts[1:]] + [far]
        left = [(b, -ends[b], -starts[b]) for b in range(len(starts))][::-1]
        right = [(BUCKETS // 2 + b, starts[b], ends[b]) for b in range(1, len(starts))]
        return left + right
    starts = side_starts(BUCKETS)
    ends = [s - 1 for s in starts[1:]] + [far]
    return [(b, -ends[b], -starts[b]) for b in range(len(starts))][::-1]

def head_mask(shape, head, size):
    lane = lax.broadcasted_iota(jnp.int32, shape, 1)
    return (lane >= head * size) & (lane < (head + 1) * size)

def fill_strip(strip, table, kind, block, length):
    heads = strip.shape[0]
    offset = length - block
    ranges = bucket_ranges(kind)
    low, high = offset - 128, offset + block + 128
    width = strip.shape[2]
    lo, hi = max(low, 0), min(high, width)
    r = (lax.broadcasted_iota(jnp.int32, (block, hi - lo), 1) + (lo - offset)
         - lax.broadcasted_iota(jnp.int32, (block, hi - lo), 0))
    masks = [r >= first for _, first, _ in ranges[1:]]
    for head in range(heads):
        value = jnp.full((block, hi - lo), table[ranges[0][0], head], jnp.float32)
        for mask, (bucket, _, _) in zip(masks, ranges[1:]):
            value = jnp.where(mask, table[bucket, head], value)
        if kind == "decoder":
            value = jnp.where(r > 0, NEG, value)
        strip[head, :, lo:hi] = value
        if lo > 0:
            strip[head, :, 0:lo] = jnp.full((block, lo), table[ranges[0][0], head], jnp.float32)
        if hi < width:
            strip[head, :, hi:] = jnp.full((block, width - hi), NEG if kind == "decoder" else table[ranges[-1][0], head], jnp.float32)

def nt(a, b):
    return lax.dot_general(a, b, (((1,), (1,)), ((), ())), preferred_element_type=jnp.float32)
def tn(a, b):
    return lax.dot_general(a, b, (((0,), (0,)), ((), ())), preferred_element_type=jnp.float32)
def nn(a, b):
    return lax.dot_general(a, b, (((1,), (0,)), ((), ())), preferred_element_type=jnp.float32)

def strip_slice(place, block, length):
    return pl.ds(pl.multiple_of((length - block) - place * block, 128), length)

def forward_kernel(kind, heads, size, chunk, places, q, k, v, seg_q, seg_k, *rest):
    if kind == "cross":
        table = strip = None
        out, totals, scores, probs = rest
    else:
        table, out, totals, scores, probs, strip = rest
    block, length = q.shape[0], k.shape[0]
    step = pl.program_id(0)
    if strip is not None:
        @pl.when(step == 0)
        def _():
            fill_strip(strip, table, kind, block, length)
        window = strip_slice(places[step], block, length)
    total = jnp.zeros((block, heads * size), jnp.float32)
    queries = q[...]
    for head in range(heads):
        mask = head_mask(queries.shape, head, size)
        scores[head] = nt(jnp.where(mask, queries, 0).astype(jnp.bfloat16), k[...])

        def rows_step(index, carry):
            rows = pl.ds(index * chunk, chunk)
            s = scores[head, rows, :]
            if strip is not None:
                s = s + strip[head, rows, window]
            s = jnp.where(seg_q[rows, :] == seg_k[...], s, NEG)
            peak = jnp.max(s, axis=-1, keepdims=True)
            e = jnp.exp(s - peak)
            weight = jnp.sum(e, axis=-1, keepdims=True)
            probs[head, rows, :] = (e * (1.0 / weight)).astype(jnp.bfloat16)
            lane = lax.broadcasted_iota(jnp.int32, (chunk, 128), 1)
            here = peak + jnp.log(weight)
            if head == 0:
                totals[rows, :] = jnp.broadcast_to(here, (chunk, 128))
            else:
                totals[rows, :] = jnp.where(lane == head, here, totals[rows, :])
            return carry
        [rows_step(index, 0) for index in range(block // chunk)]
        total += jnp.where(mask, nn(probs[head], v[...]), 0.0)
    out[...] = total.astype(jnp.bfloat16)

def backward_kernel(kind, heads, size, chunk, key_block, places, q, k, v, seg_q, seg_k, dout, totals, *rest):
    if kind == "cross":
        table = strip = gsum = table_grad = None
        dq, dk, dv, scores, dprobs, probs, dscores, dk_sum, dv_sum = rest
    else:
        table, dq, dk, dv, table_grad, scores, dprobs, probs, dscores, dk_sum, dv_sum, strip, gsum = rest
    block, length = q.shape[0], k.shape[0]
    step = pl.program_id(0)
    steps = pl.num_programs(0)

    @pl.when(step == 0)
    def _():
        dk_sum[...] = jnp.zeros_like(dk_sum)
        dv_sum[...] = jnp.zeros_like(dv_sum)
        if strip is not None:
            gsum[...] = jnp.zeros_like(gsum)
            fill_strip(strip, table, kind, block, length)
    if strip is not None:
        window = strip_slice(places[step], block, length)
    total = jnp.zeros((block, heads * size), jnp.float32)
    queries = q[...]
    grads = dout[...]
    for head in range(heads):
        mask = head_mask(queries.shape, head, size)
        query = jnp.where(mask, queries, 0).astype(jnp.bfloat16)
        grad = jnp.where(mask, grads, 0).astype(jnp.bfloat16)
        scores[head] = nt(query, k[...])
        dprobs[head] = nt(grad, v[...])

        def rows_step(index, carry):
            rows = pl.ds(index * chunk, chunk)
            s = scores[head, rows, :]
            if strip is not None:
                s = s + strip[head, rows, window]
            s = jnp.where(seg_q[rows, :] == seg_k[...], s, NEG)
            p = jnp.exp(s - totals[rows, head:head + 1])
            probs[head, rows, :] = p.astype(jnp.bfloat16)
            dp = dprobs[head, rows, :]
            delta = jnp.sum(p * dp, axis=-1, keepdims=True)
            ds = (p * (dp - delta)).astype(jnp.bfloat16)
            dscores[head, rows, :] = ds
            if strip is not None:
                gsum[head, rows, window] += ds.astype(jnp.float32)
            return carry
        [rows_step(index, 0) for index in range(block // chunk)]
        ds = dscores[head]
        total += jnp.where(mask, nn(ds, k[...]), 0.0)
        dk_sum[...] += tn(ds, query)
        dv_sum[...] += tn(probs[head], grad)
    dq[...] = total.astype(jnp.bfloat16)

    @pl.when(step == steps - 1)
    def _():
        for index in range(length // key_block):
            rows = pl.ds(pl.multiple_of(places[index] * key_block, key_block), key_block)
            to = pl.ds(index * key_block, key_block)
            dk[to, :] = dk_sum[rows, :].astype(jnp.bfloat16)
            dv[to, :] = dv_sum[rows, :].astype(jnp.bfloat16)
        if strip is not None:
            table_grad[...] = bucket_sums(gsum, kind, block, length)

def bucket_sums(gsum, kind, block, length):
    heads, _, width = gsum.shape
    offset = length - block
    lo, hi = offset - 128, min(offset + block + 128, width)
    wide = block + 512
    lines = []
    for head in range(heads):
        left = None
        if lo < 0:
            g = jnp.concatenate([jnp.zeros((block, -lo), jnp.float32), gsum[head, :, 0:hi]], axis=1)
        else:
            g = gsum[head, :, lo:hi]
            if lo > 0:
                left = jnp.sum(jnp.sum(gsum[head, :, 0:lo], axis=0, keepdims=True), axis=1, keepdims=True)
        right = None
        if hi < width:
            right = jnp.sum(jnp.sum(gsum[head, :, hi:], axis=0, keepdims=True), axis=1, keepdims=True)
        g = jnp.concatenate([g, jnp.zeros((block, wide - g.shape[1]), jnp.float32)], axis=1)
        half = block // 2
        while half >= 1:
            g = g[:half] + pltpu.roll(g[half:], wide - half, 1)
            half //= 2
        lane = lax.broadcasted_iota(jnp.int32, (1, wide), 1)
        if left is not None:
            g = g + jnp.where(lane == 0, left, 0.0)
        if right is not None:
            g = g + jnp.where(lane == 256, right, 0.0)
        lines.append(g)
    line = jnp.concatenate(lines + [jnp.zeros((8 - heads, wide), jnp.float32)], axis=0)
    at = lax.broadcasted_iota(jnp.int32, (wide, 128), 0)
    r = jnp.where(at > block + 255, at - wide, at) - 128
    lane = lax.broadcasted_iota(jnp.int32, (1, 128), 1)
    first = jnp.full((1, 128), 1 << 24, jnp.int32)
    last = jnp.full((1, 128), -(1 << 24), jnp.int32)
    for bucket, a, b in bucket_ranges(kind):
        first = jnp.where(lane == bucket, a, first)
        last = jnp.where(lane == bucket, b, last)
    member = jnp.where((r >= first) & (r <= last), 1.0, 0.0)
    return lax.dot_general(line, member, (((1,), (0,)), ((), ())), precision=lax.Precision.HIGHEST, preferred_element_type=jnp.float32)

def attention_forward(kind, heads, places, q, k, v, seg_q, seg_k, table, block, chunk=32):
    n = places.shape[0]
    length, inner = k.shape
    size = inner // heads
    full = lambda shape: pl.BlockSpec(shape, lambda i, p: (0, 0))
    at = lambda cols: pl.BlockSpec((block, cols), lambda i, p: (p[i], 0))
    put = lambda cols: pl.BlockSpec((block, cols), lambda i, p: (i, 0))
    ins = [at(inner), full((length, inner)), full((length, inner)), at(1), full((1, length))]
    args = [q, k, v, seg_q, seg_k]
    scratch = [pltpu.VMEM((heads, block, length), jnp.float32), pltpu.VMEM((heads, block, length), jnp.bfloat16)]
    if kind != "cross":
        ins.append(pl.BlockSpec(memory_space=pltpu.SMEM)); args.append(table)
        scratch.append(pltpu.VMEM((heads, block, 2 * length - block), jnp.float32))
    return pl.pallas_call(
        functools.partial(forward_kernel, kind, heads, size, chunk),
        grid_spec=pltpu.PrefetchScalarGridSpec(num_scalar_prefetch=1, grid=(n,), in_specs=ins,
            out_specs=[put(inner), put(128)], scratch_shapes=scratch),
        out_shape=[jax.ShapeDtypeStruct((n * block, inner), jnp.bfloat16), jax.ShapeDtypeStruct((n * block, 128), jnp.float32)],
        cost_estimate=pl.CostEstimate(flops=n * block * length * heads * 64 * 4 * 4, bytes_accessed=n * block * inner * 8, transcendentals=n * block * length * heads),
        compiler_params=pltpu.CompilerParams(dimension_semantics=("arbitrary",), vmem_limit_bytes=VMEM_BYTES),
        name="attention_forward_" + kind,
    )(places, *args)

def attention_backward(kind, heads, places, q, k, v, seg_q, seg_k, dout, totals, table, block, key_block, chunk=32):
    n = places.shape[0]
    length, inner = k.shape
    size = inner // heads
    full = lambda shape: pl.BlockSpec(shape, lambda i, p: (0, 0))
    at = lambda cols: pl.BlockSpec((block, cols), lambda i, p: (p[i], 0))
    put = lambda cols: pl.BlockSpec((block, cols), lambda i, p: (i, 0))
    ins = [at(inner), full((length, inner)), full((length, inner)), at(1), full((1, length)), put(inner), put(128)]
    args = [q, k, v, seg_q, seg_k, dout, totals]
    outs = [put(inner), full((length, inner)), full((length, inner))]
    shapes = [jax.ShapeDtypeStruct((n * block, inner), jnp.bfloat16), jax.ShapeDtypeStruct((length, inner), jnp.bfloat16), jax.ShapeDtypeStruct((length, inner), jnp.bfloat16)]
    scratch = [pltpu.VMEM((heads, block, length), jnp.float32)] * 2 + [pltpu.VMEM((heads, block, length), jnp.bfloat16)] * 2 + [pltpu.VMEM((length, inner), jnp.float32)] * 2
    if kind != "cross":
        ins.append(pl.BlockSpec(memory_space=pltpu.SMEM)); args.append(table)
        outs.append(full((8, 128))); shapes.append(jax.ShapeDtypeStruct((8, 128), jnp.float32))
        scratch += [pltpu.VMEM((heads, block, 2 * length - block), jnp.float32)] * 2
    return pl.pallas_call(
        functools.partial(backward_kernel, kind, heads, size, chunk, key_block),
        grid_spec=pltpu.PrefetchScalarGridSpec(num_scalar_prefetch=1, grid=(n,), in_specs=ins, out_specs=outs, scratch_shapes=scratch),
        out_shape=shapes,
        cost_estimate=pl.CostEstimate(flops=n * block * length * heads * 64 * 4 * 10, bytes_accessed=n * block * inner * 16, transcendentals=n * block * length * heads),
        compiler_params=pltpu.CompilerParams(dimension_semantics=("arbitrary",), vmem_limit_bytes=VMEM_BYTES),
        name="attention_backward_" + kind,
    )(places, *args)


def normalize(residual, gain_row):
    scale_row = lax.rsqrt(jnp.mean(residual * residual, axis=-1, keepdims=True) + EPS)
    return (residual * scale_row * gain_row, scale_row)


def normalize_backward(residual, scale_row, gain_row, normed_grad):
    weighted = normed_grad * gain_row
    inner_mean = jnp.mean(residual * weighted, axis=-1, keepdims=True)
    input_grad = scale_row * weighted - residual * scale_row**3 * inner_mean
    gain_grad = jnp.sum(normed_grad * residual * scale_row, axis=0)
    return (input_grad, gain_grad)


CORE = [(0, 1), (1, 0), (2, 3), (3, 2)]
CHIP = [(0, 2), (2, 0), (1, 3), (3, 1)]


def swap_core(value):
    return lax.ppermute(value, "tensor", CORE)


def swap_chip(value):
    return lax.ppermute(value, "tensor", CHIP)


def gather_rows(rows):
    across = swap_chip(rows)
    near = jnp.concatenate([rows, swap_core(rows)], axis=0)
    far = jnp.concatenate([across, swap_core(across)], axis=0)
    return near, far


def scatter_rows(near, far):
    half = near.shape[0] // 2
    sent = far[:half] + swap_core(far[half:])
    across = swap_chip(sent.astype(jnp.bfloat16))
    return near[:half] + swap_core(near[half:]) + across.astype(jnp.float32)


def reduce_pieces(grad, size):
    place = lax.axis_index("dp")
    bits = [1 << bit for bit in range(size.bit_length() - 1)]
    current = grad
    for bit in bits:
        upper = (place // bit) % 2
        half = current.shape[0] // 2
        send = lax.dynamic_slice_in_dim(current, (1 - upper) * half, half, 0)
        keep = lax.dynamic_slice_in_dim(current, upper * half, half, 0)
        came = lax.ppermute(send, "dp", [(i, i ^ bit) for i in range(size)])
        current = (keep.astype(jnp.float32) + came.astype(jnp.float32)).astype(jnp.bfloat16)
    for bit in bits[::-1]:
        upper = (place // bit) % 2 == 1
        came = lax.ppermute(current, "dp", [(i, i ^ bit) for i in range(size)])
        current = jnp.concatenate([jnp.where(upper, came, current), jnp.where(upper, current, came)], axis=0)
    return current


def sum_all(value, size, axes):
    for axis, count in axes:
        bit = 1
        while bit < count:
            value = value + lax.ppermute(value, axis, [(i, i ^ bit) for i in range(count)])
            bit *= 2
    return value


def dot_nt(a, b):
    return lax.dot_general(a, b, (((1,), (1,)), ((), ())), preferred_element_type=jnp.float32)


def dot_nn(a, b):
    return lax.dot_general(a, b, (((1,), (0,)), ((), ())), preferred_element_type=jnp.float32)


def dot_tn(a, b):
    return lax.dot_general(a, b, (((0,), (0,)), ((), ())), preferred_element_type=jnp.float32)


def both(pair, function):
    return function(pair[0]), function(pair[1])


def to_order(value, places, block):
    out = jnp.zeros_like(value)
    for index in range(4):
        out = lax.dynamic_update_slice_in_dim(out, value[index * block:(index + 1) * block], places[index] * block, 0)
    return out


def low(value):
    return value.astype(jnp.bfloat16)


def feed_forward(normed, gate_up, down):
    gu = both(normed, lambda a: dot_nn(a, gate_up))
    hidden = both(gu, lambda x: low(jax.nn.gelu(x[:, :x.shape[1] // 2]) * x[:, x.shape[1] // 2:]))
    part = both(hidden, lambda h: dot_nn(h, down))
    return scatter_rows(*part), gu, hidden


def feed_backward(normed, gate_up, down, gu, hidden, grads):
    def one(index):
        hidden_grad = dot_nt(grads[index], down)
        gate, up = jnp.split(gu[index], 2, axis=1)
        activated, pullback = jax.vjp(jax.nn.gelu, gate)
        gate_grad = pullback(hidden_grad * up)[0]
        return low(jnp.concatenate([gate_grad, hidden_grad * activated], axis=1))
    stacked = one(0), one(1)
    normed_grad = scatter_rows(*both(stacked, lambda s: dot_nt(s, gate_up)))
    join = lambda pair: jnp.concatenate(pair, axis=0)
    rows, cols = join(normed), join(stacked)
    gate_up_grad = low(dot_tn(rows, cols))
    down_grad = low(dot_tn(join(hidden), join(grads)))
    return normed_grad, gate_up_grad, down_grad


def local(
    sizes,
    encoder_rows,
    decoder_rows,
    encoder_segments,
    decoder_segments,
    norm_gains,
    encoder_attention_in,
    encoder_attention_out,
    encoder_gate_up,
    encoder_down,
    decoder_attention_in,
    decoder_attention_out,
    cross_queries,
    cross_key_value_rows,
    cross_output,
    decoder_gate_up,
    decoder_down,
    position_tables,
    encoder_cotangent,
    decoder_cotangent,
):
    dp = sizes["dp"]
    heads = position_tables.shape[2]
    inner = cross_output.shape[0]
    width = encoder_rows.shape[1]
    eb, db = encoder_rows.shape[0], decoder_rows.shape[0]
    t = lax.axis_index("tensor").astype(jnp.int32)
    places = jnp.bitwise_xor(t, jnp.arange(4, dtype=jnp.int32))
    weight_in = lambda w: jnp.transpose(w, (1, 2, 0)).reshape(-1, width)
    enc_in, dec_in, kv_in = weight_in(encoder_attention_in), weight_in(decoder_attention_in), weight_in(cross_key_value_rows)
    q_in = jnp.transpose(cross_queries)
    enc_gu = encoder_gate_up.reshape(width, -1)
    dec_gu = decoder_gate_up.reshape(width, -1)
    enc_seg_k, dec_seg_k = encoder_segments, decoder_segments
    enc_seg_q, dec_seg_q = jnp.transpose(encoder_segments), jnp.transpose(decoder_segments)
    join = lambda pair: jnp.concatenate(pair, axis=0)

    def project(pair, weight, block):
        rows = join(pair)
        return [to_order(low(dot_nt(rows, weight[i:i + inner])), places, block) for i in range(0, weight.shape[0], inner)]

    def out_part(attended, weight):
        half = attended.shape[0] // 2
        return scatter_rows(dot_nn(attended[:half], weight), dot_nn(attended[half:], weight))

    x = encoder_rows.astype(jnp.float32)
    y = decoder_rows.astype(jnp.float32)
    normed, enc_s0 = normalize(x, norm_gains[0])
    enc_a0 = gather_rows(low(normed))
    normed, dec_s3 = normalize(y, norm_gains[3])
    dec_a3 = gather_rows(low(normed))
    qkv1 = project(enc_a0, enc_in, eb)
    att1, tot1 = attention_forward("encoder", heads, places, *qkv1, enc_seg_q, enc_seg_k, position_tables[0], eb, chunk=64)
    h = x + out_part(att1, encoder_attention_out)
    normed, enc_s1 = normalize(h, norm_gains[1])
    enc_a1 = gather_rows(low(normed))
    qkv2 = project(dec_a3, dec_in, db)
    att2, tot2 = attention_forward("decoder", heads, places, *qkv2, dec_seg_q, dec_seg_k, position_tables[1], db, chunk=db)
    part, gu1, hid1 = feed_forward(enc_a1, enc_gu, encoder_down)
    e = h + part
    normed, enc_s2 = normalize(e, norm_gains[2])
    encoder_result = low(normed)
    enc_r = gather_rows(encoder_result)
    m = y + out_part(att2, decoder_attention_out)
    normed, dec_s4 = normalize(m, norm_gains[4])
    dec_a4 = gather_rows(low(normed))
    cq = project(dec_a4, q_in, db)[0]
    ck, cv = project(enc_r, kv_in, eb)
    att3, tot3 = attention_forward("cross", heads, places, cq, ck, cv, dec_seg_q, enc_seg_k, None, db, chunk=db)
    n = m + out_part(att3, cross_output)
    normed, dec_s5 = normalize(n, norm_gains[5])
    dec_a5 = gather_rows(low(normed))
    part, gu2, hid2 = feed_forward(dec_a5, dec_gu, decoder_down)
    decoder_result = low(n + part)

    result_grad = decoder_cotangent.astype(jnp.float32)
    grads = gather_rows(decoder_cotangent)
    normed_grad, dec_gu_grad, dec_down_grad = feed_backward(dec_a5, dec_gu, decoder_down, gu2, hid2, grads)
    part, gain5 = normalize_backward(n, dec_s5, norm_gains[5], normed_grad)
    later_grad = result_grad + part
    grads = gather_rows(low(later_grad))
    co_grad = low(dot_nt(join(grads), cross_output))
    cross_output_grad = low(dot_tn(att3, join(grads)))
    dcq, dck, dcv = attention_backward("cross", heads, places, cq, ck, cv, dec_seg_q, enc_seg_k, co_grad, tot3, None, db, eb, chunk=db)
    half = 2 * eb
    kv_grad = jnp.concatenate([dck, dcv], axis=1)
    kv_normed = scatter_rows(dot_nn(kv_grad[:half], kv_in), dot_nn(kv_grad[half:], kv_in))
    q_normed = scatter_rows(dot_nn(dcq[:2 * db], q_in), dot_nn(dcq[2 * db:], q_in))
    cross_queries_grad = low(dot_tn(dcq, join(dec_a4)))
    cross_kv_grad = low(dot_tn(kv_grad, join(enc_r)))
    part, gain2 = normalize_backward(e, enc_s2, norm_gains[2], encoder_cotangent.astype(jnp.float32) + kv_normed)
    last_grad = part
    grads = gather_rows(low(last_grad))
    normed_grad, enc_gu_grad, enc_down_grad = feed_backward(enc_a1, enc_gu, encoder_down, gu1, hid1, grads)
    part, gain4 = normalize_backward(m, dec_s4, norm_gains[4], q_normed)
    middle_grad = later_grad + part
    dec_grads = gather_rows(low(middle_grad))

    def self_backward(kind, grads, weight_in, weight_out, qkv, attended, totals, seg_q, seg_k, table, block, normed, chunk):
        rows = join(grads)
        out_grad = low(dot_nt(rows, weight_out))
        dq, dk, dv, table_grad = attention_backward(kind, heads, places, *qkv, seg_q, seg_k, out_grad, totals, table, block, block, chunk=chunk)
        dqkv = jnp.concatenate([dq, dk, dv], axis=1)
        normed_grad = scatter_rows(dot_nn(dqkv[:2 * block], weight_in), dot_nn(dqkv[2 * block:], weight_in))
        return normed_grad, low(dot_tn(dqkv, join(normed))), low(dot_tn(attended, rows)), table_grad[:heads, :BUCKETS]

    part, gain1 = normalize_backward(h, enc_s1, norm_gains[1], normed_grad)
    h_grad = last_grad + part
    grads = gather_rows(low(h_grad))
    normed_grad, dec_in_grad, dec_out_grad, dec_table = self_backward(
        "decoder", dec_grads, dec_in, decoder_attention_out, qkv2, att2, tot2, dec_seg_q, dec_seg_k, position_tables[1], db, dec_a3, db)
    part, gain3 = normalize_backward(y, dec_s3, norm_gains[3], normed_grad)
    decoder_rows_gradient = middle_grad + part
    normed_grad, enc_in_grad, enc_out_grad, enc_table = self_backward(
        "encoder", grads, enc_in, encoder_attention_out, qkv1, att1, tot1, enc_seg_q, enc_seg_k, position_tables[0], eb, enc_a0, 64)
    part, gain0 = normalize_backward(x, enc_s0, norm_gains[0], normed_grad)
    encoder_rows_gradient = h_grad + part

    wide = lambda a: a.astype(jnp.float32)
    total = functools.partial(reduce_pieces, size=dp)
    dec_gu_sum, dec_down_sum = wide(total(dec_gu_grad)), wide(total(dec_down_grad))
    cross = total(jnp.concatenate([cross_output_grad, cross_queries_grad, cross_kv_grad], axis=0))
    enc_gu_sum, enc_down_sum = wide(total(enc_gu_grad)), wide(total(enc_down_grad))
    dec_att = total(jnp.concatenate([dec_out_grad, dec_in_grad], axis=0))
    enc_att = total(jnp.concatenate([enc_out_grad, enc_in_grad], axis=0))
    gains = jnp.stack([gain0, gain1, gain2, gain3, gain4, gain5])
    gains = sum_all(gains, None, [("tensor", 4)])
    tables = jnp.stack([enc_table, dec_table])
    small = jnp.concatenate([gains.reshape(-1), tables.reshape(-1)])
    small = sum_all(small, None, [("dp", dp)])
    gains = small[:gains.size].reshape(gains.shape)
    tables = small[gains.size:].reshape(tables.shape)
    unfold = lambda g, parts: jnp.transpose(wide(g).reshape(parts, inner, width), (2, 0, 1))
    return (
        encoder_result,
        decoder_result,
        encoder_rows_gradient,
        decoder_rows_gradient,
        gains,
        unfold(enc_att[inner:], 3),
        wide(enc_att[:inner]),
        enc_gu_sum.reshape(encoder_gate_up.shape),
        enc_down_sum,
        unfold(dec_att[inner:], 3),
        wide(dec_att[:inner]),
        jnp.transpose(wide(cross[inner:2 * inner])),
        unfold(cross[2 * inner:], 2),
        wide(cross[:inner]),
        dec_gu_sum.reshape(decoder_gate_up.shape),
        dec_down_sum,
        jnp.transpose(tables, (0, 2, 1)),
    )


def solution(mesh):
    return jax.shard_map(
        functools.partial(local, dict(mesh.shape)),
        mesh=mesh,
        in_specs=(
            P(("dp", "tensor"), None),
            P(("dp", "tensor"), None),
            P("dp", None),
            P("dp", None),
            P(),
            P(None, None, "tensor"),
            P("tensor", None),
            P(None, None, "tensor"),
            P("tensor", None),
            P(None, None, "tensor"),
            P("tensor", None),
            P(None, "tensor"),
            P(None, None, "tensor"),
            P("tensor", None),
            P(None, None, "tensor"),
            P("tensor", None),
            P(None, None, "tensor"),
            P(("dp", "tensor"), None),
            P(("dp", "tensor"), None),
        ),
        out_specs=(
            P(("dp", "tensor"), None),
            P(("dp", "tensor"), None),
            P(("dp", "tensor"), None),
            P(("dp", "tensor"), None),
            P(),
            P(None, None, "tensor"),
            P("tensor", None),
            P(None, None, "tensor"),
            P("tensor", None),
            P(None, None, "tensor"),
            P("tensor", None),
            P(None, "tensor"),
            P(None, None, "tensor"),
            P("tensor", None),
            P(None, None, "tensor"),
            P("tensor", None),
            P(None, None, "tensor"),
        ),
        check_vma=False,
    )
```

```python
import functools, math
import jax
import jax.numpy as jnp
from jax import lax
from jax.experimental import pallas as pl
from jax.experimental.pallas import tpu as pltpu
from jax.sharding import PartitionSpec as P

BUCKETS = 32
EPS = 1e-06
NEG = -1e30
VMEM_BYTES = 56 * 2**20


def bucket_limits(exact_range, far_range, bucket_count):
    limits = []
    for level_index in range(1, bucket_count - exact_range):
        candidate = exact_range
        while (int(math.log(candidate / exact_range) / math.log(far_range / exact_range) * (bucket_count - exact_range)) < level_index):
            candidate += 1
        limits.append(candidate)
    return limits

def side_starts(count):
    exact = count // 2
    return list(range(exact + 1)) + bucket_limits(exact, 128, count)

def bucket_ranges(kind):
    far = 1 << 20
    if kind == "encoder":
        starts = side_starts(BUCKETS // 2)
        ends = [s - 1 for s in starts[1:]] + [far]
        left = [(b, -ends[b], -starts[b]) for b in range(len(starts))][::-1]
        right = [(BUCKETS // 2 + b, starts[b], ends[b]) for b in range(1, len(starts))]
        return left + right
    starts = side_starts(BUCKETS)
    ends = [s - 1 for s in starts[1:]] + [far]
    return [(b, -ends[b], -starts[b]) for b in range(len(starts))][::-1]

def head_mask(shape, head, size):
    lane = lax.broadcasted_iota(jnp.int32, shape, 1)
    return (lane >= head * size) & (lane < (head + 1) * size)

def fill_strip(strip, table, kind, block, length):
    heads = strip.shape[0]
    offset = length - block
    ranges = bucket_ranges(kind)
    low, high = offset - 128, offset + block + 128
    width = strip.shape[2]
    lo, hi = max(low, 0), min(high, width)
    r = (lax.broadcasted_iota(jnp.int32, (block, hi - lo), 1) + (lo - offset)
         - lax.broadcasted_iota(jnp.int32, (block, hi - lo), 0))
    masks = [r >= first for _, first, _ in ranges[1:]]
    for head in range(heads):
        value = jnp.full((block, hi - lo), table[ranges[0][0], head], jnp.float32)
        for mask, (bucket, _, _) in zip(masks, ranges[1:]):
            value = jnp.where(mask, table[bucket, head], value)
        if kind == "decoder":
            value = jnp.where(r > 0, NEG, value)
        strip[head, :, lo:hi] = value
        if lo > 0:
            strip[head, :, 0:lo] = jnp.full((block, lo), table[ranges[0][0], head], jnp.float32)
        if hi < width:
            strip[head, :, hi:] = jnp.full((block, width - hi), NEG if kind == "decoder" else table[ranges[-1][0], head], jnp.float32)

def nt(a, b):
    return lax.dot_general(a, b, (((1,), (1,)), ((), ())), preferred_element_type=jnp.float32)
def tn(a, b):
    return lax.dot_general(a, b, (((0,), (0,)), ((), ())), preferred_element_type=jnp.float32)
def nn(a, b):
    return lax.dot_general(a, b, (((1,), (0,)), ((), ())), preferred_element_type=jnp.float32)

def strip_slice(place, block, length):
    return pl.ds(pl.multiple_of((length - block) - place * block, 128), length)

def forward_kernel(kind, heads, size, chunk, places, q, k, v, seg_q, seg_k, *rest):
    if kind == "cross":
        table = strip = None
        out, totals, scores, probs = rest
    else:
        table, out, totals, scores, probs, strip = rest
    block, length = q.shape[0], k.shape[0]
    step = pl.program_id(0)
    if strip is not None:
        @pl.when(step == 0)
        def _():
            fill_strip(strip, table, kind, block, length)
        window = strip_slice(places[step], block, length)
    total = jnp.zeros((block, heads * size), jnp.float32)
    queries = q[...]
    for head in range(heads):
        mask = head_mask(queries.shape, head, size)
        scores[head] = nt(jnp.where(mask, queries, 0).astype(jnp.bfloat16), k[...])

        def rows_step(index, carry):
            rows = pl.ds(index * chunk, chunk)
            s = scores[head, rows, :]
            if strip is not None:
                s = s + strip[head, rows, window]
            s = jnp.where(seg_q[rows, :] == seg_k[...], s, NEG)
            peak = jnp.max(s, axis=-1, keepdims=True)
            e = jnp.exp(s - peak)
            weight = jnp.sum(e, axis=-1, keepdims=True)
            probs[head, rows, :] = (e * (1.0 / weight)).astype(jnp.bfloat16)
            lane = lax.broadcasted_iota(jnp.int32, (chunk, 128), 1)
            here = peak + jnp.log(weight)
            if head == 0:
                totals[rows, :] = jnp.broadcast_to(here, (chunk, 128))
            else:
                totals[rows, :] = jnp.where(lane == head, here, totals[rows, :])
            return carry
        [rows_step(index, 0) for index in range(block // chunk)]
        total += jnp.where(mask, nn(probs[head], v[...]), 0.0)
    out[...] = total.astype(jnp.bfloat16)

def backward_kernel(kind, heads, size, chunk, key_block, places, q, k, v, seg_q, seg_k, dout, totals, *rest):
    if kind == "cross":
        table = strip = gsum = table_grad = None
        dq, dk, dv, scores, dprobs, probs, dscores, dk_sum, dv_sum = rest
    else:
        table, dq, dk, dv, table_grad, scores, dprobs, probs, dscores, dk_sum, dv_sum, strip, gsum = rest
    block, length = q.shape[0], k.shape[0]
    step = pl.program_id(0)
    steps = pl.num_programs(0)

    @pl.when(step == 0)
    def _():
        dk_sum[...] = jnp.zeros_like(dk_sum)
        dv_sum[...] = jnp.zeros_like(dv_sum)
        if strip is not None:
            gsum[...] = jnp.zeros_like(gsum)
            fill_strip(strip, table, kind, block, length)
    if strip is not None:
        window = strip_slice(places[step], block, length)
    total = jnp.zeros((block, heads * size), jnp.float32)
    queries = q[...]
    grads = dout[...]
    for head in range(heads):
        mask = head_mask(queries.shape, head, size)
        query = jnp.where(mask, queries, 0).astype(jnp.bfloat16)
        grad = jnp.where(mask, grads, 0).astype(jnp.bfloat16)
        scores[head] = nt(query, k[...])
        dprobs[head] = nt(grad, v[...])

        def rows_step(index, carry):
            rows = pl.ds(index * chunk, chunk)
            s = scores[head, rows, :]
            if strip is not None:
                s = s + strip[head, rows, window]
            s = jnp.where(seg_q[rows, :] == seg_k[...], s, NEG)
            p = jnp.exp(s - totals[rows, head:head + 1])
            probs[head, rows, :] = p.astype(jnp.bfloat16)
            dp = dprobs[head, rows, :]
            delta = jnp.sum(p * dp, axis=-1, keepdims=True)
            ds = (p * (dp - delta)).astype(jnp.bfloat16)
            dscores[head, rows, :] = ds
            if strip is not None:
                gsum[head, rows, window] += ds.astype(jnp.float32)
            return carry
        [rows_step(index, 0) for index in range(block // chunk)]
        ds = dscores[head]
        total += jnp.where(mask, nn(ds, k[...]), 0.0)
        dk_sum[...] += tn(ds, query)
        dv_sum[...] += tn(probs[head], grad)
    dq[...] = total.astype(jnp.bfloat16)

    @pl.when(step == steps - 1)
    def _():
        for index in range(length // key_block):
            rows = pl.ds(pl.multiple_of(places[index] * key_block, key_block), key_block)
            to = pl.ds(index * key_block, key_block)
            dk[to, :] = dk_sum[rows, :].astype(jnp.bfloat16)
            dv[to, :] = dv_sum[rows, :].astype(jnp.bfloat16)
        if strip is not None:
            table_grad[...] = bucket_sums(gsum, kind, block, length)

def bucket_sums(gsum, kind, block, length):
    heads, _, width = gsum.shape
    offset = length - block
    lo, hi = offset - 128, min(offset + block + 128, width)
    wide = block + 512
    lines = []
    for head in range(heads):
        left = None
        if lo < 0:
            g = jnp.concatenate([jnp.zeros((block, -lo), jnp.float32), gsum[head, :, 0:hi]], axis=1)
        else:
            g = gsum[head, :, lo:hi]
            if lo > 0:
                left = jnp.sum(jnp.sum(gsum[head, :, 0:lo], axis=0, keepdims=True), axis=1, keepdims=True)
        right = None
        if hi < width:
            right = jnp.sum(jnp.sum(gsum[head, :, hi:], axis=0, keepdims=True), axis=1, keepdims=True)
        g = jnp.concatenate([g, jnp.zeros((block, wide - g.shape[1]), jnp.float32)], axis=1)
        half = block // 2
        while half >= 1:
            g = g[:half] + pltpu.roll(g[half:], wide - half, 1)
            half //= 2
        lane = lax.broadcasted_iota(jnp.int32, (1, wide), 1)
        if left is not None:
            g = g + jnp.where(lane == 0, left, 0.0)
        if right is not None:
            g = g + jnp.where(lane == 256, right, 0.0)
        lines.append(g)
    line = jnp.concatenate(lines + [jnp.zeros((8 - heads, wide), jnp.float32)], axis=0)
    at = lax.broadcasted_iota(jnp.int32, (wide, 128), 0)
    r = jnp.where(at > block + 255, at - wide, at) - 128
    lane = lax.broadcasted_iota(jnp.int32, (1, 128), 1)
    first = jnp.full((1, 128), 1 << 24, jnp.int32)
    last = jnp.full((1, 128), -(1 << 24), jnp.int32)
    for bucket, a, b in bucket_ranges(kind):
        first = jnp.where(lane == bucket, a, first)
        last = jnp.where(lane == bucket, b, last)
    member = jnp.where((r >= first) & (r <= last), 1.0, 0.0)
    return lax.dot_general(line, member, (((1,), (0,)), ((), ())), precision=lax.Precision.HIGHEST, preferred_element_type=jnp.float32)

def attention_forward(kind, heads, places, q, k, v, seg_q, seg_k, table, block, chunk=32):
    n = places.shape[0]
    length, inner = k.shape
    size = inner // heads
    full = lambda shape: pl.BlockSpec(shape, lambda i, p: (0, 0))
    at = lambda cols: pl.BlockSpec((block, cols), lambda i, p: (p[i], 0))
    put = lambda cols: pl.BlockSpec((block, cols), lambda i, p: (i, 0))
    ins = [at(inner), full((length, inner)), full((length, inner)), at(1), full((1, length))]
    args = [q, k, v, seg_q, seg_k]
    scratch = [pltpu.VMEM((heads, block, length), jnp.float32), pltpu.VMEM((heads, block, length), jnp.bfloat16)]
    if kind != "cross":
        ins.append(pl.BlockSpec(memory_space=pltpu.SMEM)); args.append(table)
        scratch.append(pltpu.VMEM((heads, block, 2 * length - block), jnp.float32))
    return pl.pallas_call(
        functools.partial(forward_kernel, kind, heads, size, chunk),
        grid_spec=pltpu.PrefetchScalarGridSpec(num_scalar_prefetch=1, grid=(n,), in_specs=ins,
            out_specs=[put(inner), put(128)], scratch_shapes=scratch),
        out_shape=[jax.ShapeDtypeStruct((n * block, inner), jnp.bfloat16), jax.ShapeDtypeStruct((n * block, 128), jnp.float32)],
        cost_estimate=pl.CostEstimate(flops=n * block * length * heads * 64 * 4 * 4, bytes_accessed=n * block * inner * 8, transcendentals=n * block * length * heads),
        compiler_params=pltpu.CompilerParams(dimension_semantics=("arbitrary",), vmem_limit_bytes=VMEM_BYTES),
        name="attention_forward_" + kind,
    )(places, *args)

def attention_backward(kind, heads, places, q, k, v, seg_q, seg_k, dout, totals, table, block, key_block, chunk=32):
    n = places.shape[0]
    length, inner = k.shape
    size = inner // heads
    full = lambda shape: pl.BlockSpec(shape, lambda i, p: (0, 0))
    at = lambda cols: pl.BlockSpec((block, cols), lambda i, p: (p[i], 0))
    put = lambda cols: pl.BlockSpec((block, cols), lambda i, p: (i, 0))
    ins = [at(inner), full((length, inner)), full((length, inner)), at(1), full((1, length)), put(inner), put(128)]
    args = [q, k, v, seg_q, seg_k, dout, totals]
    outs = [put(inner), full((length, inner)), full((length, inner))]
    shapes = [jax.ShapeDtypeStruct((n * block, inner), jnp.bfloat16), jax.ShapeDtypeStruct((length, inner), jnp.bfloat16), jax.ShapeDtypeStruct((length, inner), jnp.bfloat16)]
    scratch = [pltpu.VMEM((heads, block, length), jnp.float32)] * 2 + [pltpu.VMEM((heads, block, length), jnp.bfloat16)] * 2 + [pltpu.VMEM((length, inner), jnp.float32)] * 2
    if kind != "cross":
        ins.append(pl.BlockSpec(memory_space=pltpu.SMEM)); args.append(table)
        outs.append(full((8, 128))); shapes.append(jax.ShapeDtypeStruct((8, 128), jnp.float32))
        scratch += [pltpu.VMEM((heads, block, 2 * length - block), jnp.float32)] * 2
    return pl.pallas_call(
        functools.partial(backward_kernel, kind, heads, size, chunk, key_block),
        grid_spec=pltpu.PrefetchScalarGridSpec(num_scalar_prefetch=1, grid=(n,), in_specs=ins, out_specs=outs, scratch_shapes=scratch),
        out_shape=shapes,
        cost_estimate=pl.CostEstimate(flops=n * block * length * heads * 64 * 4 * 10, bytes_accessed=n * block * inner * 16, transcendentals=n * block * length * heads),
        compiler_params=pltpu.CompilerParams(dimension_semantics=("arbitrary",), vmem_limit_bytes=VMEM_BYTES),
        name="attention_backward_" + kind,
    )(places, *args)

MESH = pl.DeviceIdType.MESH


def low(value):
    return value.astype(jnp.bfloat16)


def wide(value):
    return value.astype(jnp.float32)


def root_scale(rows):
    return lax.rsqrt(jnp.mean(rows * rows, axis=-1, keepdims=True) + EPS)


def normalize(rows, gain):
    return rows * root_scale(rows) * gain


def normalize_backward(rows, gain, grad):
    scale = root_scale(rows)
    weighted = grad * gain
    inner = jnp.mean(rows * weighted, axis=-1, keepdims=True)
    gain_grad = jnp.sum(grad * rows * scale, axis=0, keepdims=True)
    return scale * weighted - rows * (scale * scale * scale) * inner, gain_grad


def gelu_parts(x):
    c = math.sqrt(2.0 / math.pi)
    square = x * x
    th = jnp.tanh(c * (x + 0.044715 * (square * x)))
    half = 0.5 * (1.0 + th)
    slope = half + 0.5 * x * (1.0 - th * th) * (c * (1.0 + 3 * 0.044715 * square))
    return x * half, slope


class Links:
    def __init__(self, send, recv):
        self.send, self.recv, self.used, self.open = send, recv, 0, []
        self.t = lax.axis_index("tensor")
        self.core = {"tensor": self.t + 1 - 2 * lax.rem(self.t, 2)}
        self.chip = {"tensor": lax.rem(self.t + 2, 4)}

    def enter(self):
        barrier = pltpu.get_barrier_semaphore()
        for peer in (self.core, self.chip):
            pl.semaphore_signal(barrier, inc=1, device_id=peer, device_id_type=MESH)
        pl.semaphore_wait(barrier, 2)

    def copy(self, source, target, peer):
        index = self.used
        self.used += 1
        made = pltpu.make_async_remote_copy(
            src_ref=source, dst_ref=target, send_sem=self.send.at[index], recv_sem=self.recv.at[index],
            device_id=peer, device_id_type=MESH)
        made.start()
        self.open.append(made)
        return made

    def close(self):
        for made in self.open:
            made.wait_send()

    def place(self, index):
        low_bit = lax.rem(self.t, 2)
        high_bit = lax.div(self.t, 2)
        if index % 2:
            low_bit = 1 - low_bit
        if index // 2:
            high_bit = 1 - high_bit
        return 2 * high_bit + low_bit


def gather(links, buf, on_near=None, on_far=None):
    block = buf.shape[0] // 4
    slot = lambda i: buf.at[pl.ds(i * block, block)]
    across = links.copy(slot(0), slot(2), links.chip)
    beside = links.copy(slot(0), slot(1), links.core)
    yield
    beside.wait_recv()
    if on_near is not None:
        on_near()
    yield
    across.wait_recv()
    passed = links.copy(slot(2), slot(3), links.core)
    yield
    passed.wait_recv()
    if on_far is not None:
        on_far()


def scatter(links, bufs, on_far, on_near, value_near=None):
    partial, came, sent, landed = bufs
    block = sent.shape[0]
    partial[2 * block:] = on_far()
    first = links.copy(partial.at[pl.ds(3 * block, block)], came.at[0], links.core)
    partial[:2 * block] = on_near()
    second = links.copy(partial.at[pl.ds(block, block)], came.at[1], links.core)
    yield
    first.wait_recv()
    sent[...] = low(partial[2 * block:3 * block] + came[0])
    across = links.copy(sent, landed, links.chip)
    yield
    second.wait_recv()
    mine = partial[:block] + came[1]
    yield
    across.wait_recv()
    return mine + wide(landed[...])


def scatter_bufs(block, width):
    return [
        pltpu.VMEM((4 * block, width), jnp.float32),
        pltpu.VMEM((2, block, width), jnp.float32),
        pltpu.VMEM((block, width), jnp.bfloat16),
        pltpu.VMEM((block, width), jnp.bfloat16),
    ]


def run(*chains):
    chains = list(chains)
    while chains:
        for chain in list(chains):
            try:
                next(chain)
            except StopIteration:
                chains.remove(chain)


def call(name, number, body, ins, outs, scratch, copies):
    n_in, n_out, n_scratch = len(ins), len(outs), len(scratch)

    def kernel(*refs):
        in_refs, refs = refs[:n_in], refs[n_in:]
        out_refs, refs = refs[:n_out], refs[n_out:]
        scratch_refs, (send, recv) = refs[:n_scratch], refs[n_scratch:]
        links = Links(send, recv)
        links.enter()
        body(links, in_refs, out_refs, scratch_refs)
        links.close()
        assert links.used == copies, links.used

    vmem = pl.BlockSpec(memory_space=pltpu.VMEM)
    return pl.pallas_call(
        kernel,
        in_specs=[vmem] * n_in,
        out_specs=[vmem] * n_out,
        out_shape=[jax.ShapeDtypeStruct(shape, dtype) for shape, dtype in outs],
        scratch_shapes=[*scratch, pltpu.SemaphoreType.DMA((copies,)), pltpu.SemaphoreType.DMA((copies,))],
        compiler_params=pltpu.CompilerParams(collective_id=number, has_side_effects=True, vmem_limit_bytes=VMEM_BYTES),
        name=name,
    )(*ins)


BF, F32 = jnp.bfloat16, jnp.float32


def project(links, rows_ref, weight, targets, first, block, inner):
    for index in (first, first + 1):
        rows = rows_ref[index * block:(index + 1) * block, :]
        at = pl.ds(pl.multiple_of(links.place(index) * block, block), block)
        for number, target in enumerate(targets):
            target[at, :] = low(nt(rows, weight[number * inner:(number + 1) * inner, :]))


def first_kernel(x, y, gains, enc_in, dec_in):
    (eb, width), db, inner = x.shape, y.shape[0], enc_in.shape[0] // 3

    def body(links, ins, outs, scratch):
        x, y, gains, enc_in, dec_in = ins
        a0, a3, q1, k1, v1, q2, k2, v2 = outs
        a0[:eb] = low(normalize(wide(x[...]), gains[0:1, :]))

        def enc():
            step = lambda first: lambda: project(links, a0, enc_in, (q1, k1, v1), first, eb, inner)
            yield from gather(links, a0, step(0), step(2))

        def dec():
            a3[:db] = low(normalize(wide(y[...]), gains[3:4, :]))
            step = lambda first: lambda: project(links, a3, dec_in, (q2, k2, v2), first, db, inner)
            yield from gather(links, a3, step(0), step(2))
        run(enc(), dec())

    outs = [((4 * eb, width), BF), ((4 * db, width), BF)] + [((4 * eb, inner), BF)] * 3 + [((4 * db, inner), BF)] * 3
    return call("rows_in", 1, body, (x, y, gains, enc_in, dec_in), outs, [], 6)


def second_kernel(att1, att2, enc_out, dec_out, x, y, gains, enc_gu, enc_down, kv_in, q_in, cot):
    (eb, width), db, inner, ff = x.shape, y.shape[0], enc_out.shape[0], enc_down.shape[0]

    def body(links, ins, outs, scratch):
        att1, att2, enc_out, dec_out, x, y, gains, enc_gu, enc_down, kv_in, q_in, cot = ins
        h_out, e_out, m_out, result, a1, gu1, hid1, closing, ck, cv, a4, cq, cot_all = outs

        def feed(first):
            for index in (first, first + 1):
                rows = slice(index * eb, (index + 1) * eb)
                gu = nn(a1[rows, :], enc_gu[...])
                gu1[rows, :] = gu
                gate, up = gu[:, :ff], gu[:, ff:]
                hid1[rows, :] = low(gelu_parts(gate)[0] * up)

        def enc():
            h = wide(x[...]) + (yield from scatter(
                links, scratch[0:4], lambda: nn(att1[2 * eb:, :], enc_out[...]), lambda: nn(att1[:2 * eb, :], enc_out[...])))
            h_out[...] = h
            a1[:eb] = low(normalize(h, gains[1:2, :]))
            yield from gather(links, a1, lambda: feed(0), lambda: feed(2))
            e = h_out[...] + (yield from scatter(
                links, scratch[4:8], lambda: nn(hid1[2 * eb:, :], enc_down[...]), lambda: nn(hid1[:2 * eb, :], enc_down[...])))
            e_out[...] = e
            closed = low(normalize(e, gains[2:3, :]))
            result[...] = closed
            closing[:eb] = closed
            step = lambda first: lambda: project(links, closing, kv_in, (ck, cv), first, eb, inner)
            yield from gather(links, closing, step(0), step(2))

        def dec():
            m = wide(y[...]) + (yield from scatter(
                links, scratch[8:12], lambda: nn(att2[2 * db:, :], dec_out[...]), lambda: nn(att2[:2 * db, :], dec_out[...])))
            m_out[...] = m
            a4[:db] = low(normalize(m, gains[4:5, :]))
            step = lambda first: lambda: project(links, a4, q_in, (cq,), first, db, inner)
            yield from gather(links, a4, step(0), step(2))
            cot_all[:db] = cot[...]
            yield from gather(links, cot_all)
        run(enc(), dec())

    outs = [((eb, width), F32), ((eb, width), F32), ((db, width), F32), ((eb, width), BF), ((4 * eb, width), BF),
            ((4 * eb, 2 * ff), F32), ((4 * eb, ff), BF), ((4 * eb, width), BF), ((4 * eb, inner), BF), ((4 * eb, inner), BF),
            ((4 * db, width), BF), ((4 * db, inner), BF), ((4 * db, width), BF)]
    scratch = scatter_bufs(eb, width) * 2 + scatter_bufs(db, width)
    return call("encoder_rows", 2, body, (att1, att2, enc_out, dec_out, x, y, gains, enc_gu, enc_down, kv_in, q_in, cot), outs, scratch, 21)


def feed_back(gu, hid, a, grads, gate_up, down, rows, stacked):
    ff = down.shape[0]
    hidden_grad = nt(grads[rows, :], down[...])
    gate, up = gu[rows, :ff], gu[rows, ff:]
    active, slope = gelu_parts(gate)
    stacked[rows, :ff] = low(hidden_grad * up * slope)
    stacked[rows, ff:] = low(hidden_grad * active)


def third_kernel(att3, cross_out, m, gains, dec_gu, dec_down, cot, cot_all):
    (db, width), inner, ff = m.shape, cross_out.shape[0], dec_down.shape[0]

    def body(links, ins, outs, scratch):
        att3, cross_out, m, gains, dec_gu, dec_down, cot, cot_all = ins
        result, later_out, do3, gu_grad, down_grad, out_grad, gain5 = outs
        n_keep, a5, gu, hid, stacked, grads = scratch[12:]

        def feed(first):
            rows = slice(first * db, (first + 2) * db)
            here = nn(a5[rows, :], dec_gu[...])
            gu[rows, :] = here
            active, slope = gelu_parts(here[:, :ff])
            up = here[:, ff:]
            hid[rows, :] = low(active * up)
            hidden_grad = nt(cot_all[rows, :], dec_down[...])
            stacked[rows, :ff] = low(hidden_grad * up * slope)
            stacked[rows, ff:] = low(hidden_grad * active)

        near, far = slice(0, 2 * db), slice(2 * db, 4 * db)
        started = []

        def back():
            n = m[...] + (yield from scatter(
                links, scratch[0:4], lambda: nn(att3[far, :], cross_out[...]), lambda: nn(att3[near, :], cross_out[...])))
            n_keep[...] = n
            a5[:db] = low(normalize(n, gains[5:6, :]))
            yield from gather(links, a5, lambda: feed(0), lambda: feed(2))
            started.append(True)
            grad = yield from scatter(
                links, scratch[4:8], lambda: nt(stacked[far, :], dec_gu[...]), lambda: nt(stacked[near, :], dec_gu[...]))
            part, gain = normalize_backward(n_keep[...], gains[5:6, :], grad)
            gain5[...] = jnp.broadcast_to(gain, gain5.shape)
            later = wide(cot[...]) + part
            later_out[...] = later
            grads[:db] = low(later)
            step = lambda rows: lambda: do3.__setitem__((rows, slice(None)), low(nt(grads[rows, :], cross_out[...])))
            yield from gather(links, grads, step(near), step(far))
            out_grad[...] = low(tn(att3[...], grads[...]))

        def rest():
            while not started:
                yield
            yield
            part = yield from scatter(
                links, scratch[8:12], lambda: nn(hid[far, :], dec_down[...]), lambda: nn(hid[near, :], dec_down[...]))
            result[...] = low(n_keep[...] + part)

        def weights():
            while not started:
                yield
            yield
            down_grad[...] = low(tn(hid[...], cot_all[...]))
            yield
            gu_grad[...] = low(tn(a5[...], stacked[...]))
        run(back(), rest(), weights())

    outs = [((db, width), BF), ((db, width), F32), ((4 * db, inner), BF), ((width, 2 * ff), BF), ((ff, width), BF), ((inner, width), BF), ((8, width), F32)]
    scratch = scatter_bufs(db, width) * 3 + [
        pltpu.VMEM((db, width), F32), pltpu.VMEM((4 * db, width), BF), pltpu.VMEM((4 * db, 2 * ff), F32),
        pltpu.VMEM((4 * db, ff), BF), pltpu.VMEM((4 * db, 2 * ff), BF), pltpu.VMEM((4 * db, width), BF)]
    return call("decoder_rows", 3, body, (att3, cross_out, m, gains, dec_gu, dec_down, cot, cot_all), outs, scratch, 15)


def fourth_kernel(dcq, dck, dcv, kv_in, q_in, e, m, h, gains, enc_cot, later, a1, gu1, hid1, enc_gu, enc_down, closing, a4, enc_out, dec_out, att1, att2):
    (eb, width), db, inner, ff = e.shape, m.shape[0], enc_out.shape[0], enc_down.shape[0]

    def body(links, ins, outs, scratch):
        dcq, dck, dcv, kv_in, q_in, e, m, h, gains, enc_cot, later, a1, gu1, hid1, enc_gu, enc_down, closing, a4, enc_out, dec_out, att1, att2 = ins
        h_grad, middle, do1, do2, kv_grad, q_grad, gu_grad, down_grad, enc_out_grad, dec_out_grad, gain_grads = outs
        last, grads1, grads0, grads_dec, stacked = scratch[16:]
        near, far = slice(0, 2 * eb), slice(2 * eb, 4 * eb)
        dnear, dfar = slice(0, 2 * db), slice(2 * db, 4 * db)
        marks = {}

        def feed(first):
            for index in (first, first + 1):
                feed_back(gu1, hid1, a1, grads1, enc_gu, enc_down, slice(index * eb, (index + 1) * eb), stacked)

        def enc():
            part = lambda rows: nn(dck[rows, :], kv_in[:inner, :]) + nn(dcv[rows, :], kv_in[inner:, :])
            grad = wide(enc_cot[...]) + (yield from scatter(links, scratch[0:4], lambda: part(far), lambda: part(near)))
            back, gain = normalize_backward(e[...], gains[2:3, :], grad)
            gain_grads[2:3, :] = gain
            last[...] = back
            grads1[:eb] = low(back)
            yield from gather(links, grads1, lambda: feed(0), lambda: feed(2))
            marks["fed"] = True
            grad = yield from scatter(links, scratch[4:8], lambda: nt(stacked[far, :], enc_gu[...]), lambda: nt(stacked[near, :], enc_gu[...]))
            back, gain = normalize_backward(h[...], gains[1:2, :], grad)
            gain_grads[1:2, :] = gain
            total = last[...] + back
            h_grad[...] = total
            grads0[:eb] = low(total)
            step = lambda rows: lambda: do1.__setitem__((rows, slice(None)), low(nt(grads0[rows, :], enc_out[...])))
            yield from gather(links, grads0, step(near), step(far))
            enc_out_grad[...] = low(tn(att1[...], grads0[...]))

        def dec():
            grad = yield from scatter(links, scratch[8:12], lambda: nn(dcq[dfar, :], q_in[...]), lambda: nn(dcq[dnear, :], q_in[...]))
            back, gain = normalize_backward(m[...], gains[4:5, :], grad)
            gain_grads[4:5, :] = gain
            total = later[...] + back
            middle[...] = total
            grads_dec[:db] = low(total)
            step = lambda rows: lambda: do2.__setitem__((rows, slice(None)), low(nt(grads_dec[rows, :], dec_out[...])))
            yield from gather(links, grads_dec, step(dnear), step(dfar))
            dec_out_grad[...] = low(tn(att2[...], grads_dec[...]))

        def weights():
            yield
            kv_grad[:inner, :] = low(tn(dck[...], closing[...]))
            yield
            kv_grad[inner:, :] = low(tn(dcv[...], closing[...]))
            q_grad[...] = low(tn(dcq[...], a4[...]))
            while "fed" not in marks:
                yield
            yield
            gu_grad[...] = low(tn(a1[...], stacked[...]))
            yield
            down_grad[...] = low(tn(hid1[...], grads1[...]))
        gain_grads[...] = jnp.zeros_like(gain_grads)
        run(enc(), dec(), weights())

    outs = [((eb, width), F32), ((db, width), F32), ((4 * eb, inner), BF), ((4 * db, inner), BF), ((2 * inner, width), BF), ((inner, width), BF),
            ((width, 2 * ff), BF), ((ff, width), BF), ((inner, width), BF), ((inner, width), BF), ((8, width), F32)]
    scratch = scatter_bufs(eb, width) * 2 + scatter_bufs(db, width) + scatter_bufs(8, 128) + [
        pltpu.VMEM((eb, width), F32), pltpu.VMEM((4 * eb, width), BF), pltpu.VMEM((4 * eb, width), BF), pltpu.VMEM((4 * db, width), BF),
        pltpu.VMEM((4 * eb, 2 * ff), BF)]
    ins = (dcq, dck, dcv, kv_in, q_in, e, m, h, gains, enc_cot, later, a1, gu1, hid1, enc_gu, enc_down, closing, a4, enc_out, dec_out, att1, att2)
    return call("encoder_back", 4, body, ins, outs, scratch, 18)


def fifth_kernel(dqkv1, dqkv2, enc_in, dec_in, x, y, gains, h_grad, middle, a0, a3):
    (eb, width), db, inner = h_grad.shape, middle.shape[0], enc_in.shape[0] // 3

    def body(links, ins, outs, scratch):
        dq1, dk1, dv1, dq2, dk2, dv2, enc_in, dec_in, x, y, gains, h_grad, middle, a0, a3 = ins
        enc_rows, dec_rows, enc_in_grad, dec_in_grad, gain_grads = outs

        def side(bufs, triple, weight, rows_in, gain_row, above, out, block):
            part = lambda rows: sum(nn(d[rows, :], weight[i * inner:(i + 1) * inner, :]) for i, d in enumerate(triple))
            grad = yield from scatter(links, bufs, lambda: part(slice(2 * block, 4 * block)), lambda: part(slice(0, 2 * block)))
            back, gain = normalize_backward(wide(rows_in[...]), gains[gain_row:gain_row + 1, :], grad)
            gain_grads[gain_row:gain_row + 1, :] = gain
            out[...] = above[...] + back

        def weights():
            for i, d in enumerate((dq1, dk1, dv1)):
                enc_in_grad[i * inner:(i + 1) * inner, :] = low(tn(d[...], a0[...]))
            yield
            for i, d in enumerate((dq2, dk2, dv2)):
                dec_in_grad[i * inner:(i + 1) * inner, :] = low(tn(d[...], a3[...]))
        gain_grads[...] = jnp.zeros_like(gain_grads)
        run(side(scratch[0:4], (dq1, dk1, dv1), enc_in, x, 0, h_grad, enc_rows, eb),
            side(scratch[4:8], (dq2, dk2, dv2), dec_in, y, 3, middle, dec_rows, db), weights())

    outs = [((eb, width), F32), ((db, width), F32), ((3 * inner, width), BF), ((3 * inner, width), BF), ((8, width), F32)]
    scratch = scatter_bufs(eb, width) + scatter_bufs(db, width)
    ins = (*dqkv1, *dqkv2, enc_in, dec_in, x, y, gains, h_grad, middle, a0, a3)
    return call("rows_back", 5, body, ins, outs, scratch, 6)


def reduce_pieces(grad, size):
    place = lax.axis_index("dp")
    bits = [1 << bit for bit in range(size.bit_length() - 1)]
    current = grad
    for bit in bits:
        upper = (place // bit) % 2
        half = current.shape[0] // 2
        send = lax.dynamic_slice_in_dim(current, (1 - upper) * half, half, 0)
        keep = lax.dynamic_slice_in_dim(current, upper * half, half, 0)
        came = lax.ppermute(send, "dp", [(i, i ^ bit) for i in range(size)])
        current = (keep.astype(jnp.float32) + came.astype(jnp.float32)).astype(jnp.bfloat16)
    for bit in bits[::-1]:
        upper = (place // bit) % 2 == 1
        came = lax.ppermute(current, "dp", [(i, i ^ bit) for i in range(size)])
        current = jnp.concatenate([jnp.where(upper, came, current), jnp.where(upper, current, came)], axis=0)
    return current


def sum_all(value, axes):
    for axis, count in axes:
        bit = 1
        while bit < count:
            value = value + lax.ppermute(value, axis, [(i, i ^ bit) for i in range(count)])
            bit *= 2
    return value


def local(
    sizes,
    encoder_rows,
    decoder_rows,
    encoder_segments,
    decoder_segments,
    norm_gains,
    encoder_attention_in,
    encoder_attention_out,
    encoder_gate_up,
    encoder_down,
    decoder_attention_in,
    decoder_attention_out,
    cross_queries,
    cross_key_value_rows,
    cross_output,
    decoder_gate_up,
    decoder_down,
    position_tables,
    encoder_cotangent,
    decoder_cotangent,
):
    dp = sizes["dp"]
    heads = position_tables.shape[2]
    inner = cross_output.shape[0]
    width = encoder_rows.shape[1]
    eb, db = encoder_rows.shape[0], decoder_rows.shape[0]
    t = lax.axis_index("tensor").astype(jnp.int32)
    places = jnp.bitwise_xor(t, jnp.arange(4, dtype=jnp.int32))
    weight_in = lambda w: jnp.transpose(w, (1, 2, 0)).reshape(-1, width)
    enc_in, dec_in, kv_in = weight_in(encoder_attention_in), weight_in(decoder_attention_in), weight_in(cross_key_value_rows)
    q_in = jnp.transpose(cross_queries)
    enc_gu = encoder_gate_up.reshape(width, -1)
    dec_gu = decoder_gate_up.reshape(width, -1)
    enc_seg_q, dec_seg_q = jnp.transpose(encoder_segments), jnp.transpose(decoder_segments)

    a0, a3, q1, k1, v1, q2, k2, v2 = first_kernel(encoder_rows, decoder_rows, norm_gains, enc_in, dec_in)
    att1, tot1 = attention_forward("encoder", heads, places, q1, k1, v1, enc_seg_q, encoder_segments, position_tables[0], eb, chunk=64)
    att2, tot2 = attention_forward("decoder", heads, places, q2, k2, v2, dec_seg_q, decoder_segments, position_tables[1], db, chunk=db)
    h, e, m, encoder_result, a1, gu1, hid1, closing, ck, cv, a4, cq, cot_all = second_kernel(
        att1, att2, encoder_attention_out, decoder_attention_out, encoder_rows, decoder_rows, norm_gains, enc_gu, encoder_down,
        kv_in, q_in, decoder_cotangent)
    att3, tot3 = attention_forward("cross", heads, places, cq, ck, cv, dec_seg_q, encoder_segments, None, db, chunk=db)
    decoder_result, later, do3, dec_gu_grad, dec_down_grad, cross_output_grad, gain5 = third_kernel(
        att3, cross_output, m, norm_gains, dec_gu, decoder_down, decoder_cotangent, cot_all)

    dcq, dck, dcv = attention_backward("cross", heads, places, cq, ck, cv, dec_seg_q, encoder_segments, do3, tot3, None, db, eb, chunk=db)
    h_grad, middle, do1, do2, cross_kv_grad, cross_queries_grad, enc_gu_grad, enc_down_grad, enc_out_grad, dec_out_grad, gains_mid = fourth_kernel(
        dcq, dck, dcv, kv_in, q_in, e, m, h, norm_gains, encoder_cotangent, later, a1, gu1, hid1, enc_gu, encoder_down, closing, a4,
        encoder_attention_out, decoder_attention_out, att1, att2)
    *dqkv2, dec_table = attention_backward(
        "decoder", heads, places, q2, k2, v2, dec_seg_q, decoder_segments, do2, tot2, position_tables[1], db, db, chunk=db)
    *dqkv1, enc_table = attention_backward(
        "encoder", heads, places, q1, k1, v1, enc_seg_q, encoder_segments, do1, tot1, position_tables[0], eb, eb, chunk=64)
    encoder_rows_gradient, decoder_rows_gradient, enc_in_grad, dec_in_grad, gains_end = fifth_kernel(
        dqkv1, dqkv2, enc_in, dec_in, encoder_rows, decoder_rows, norm_gains, h_grad, middle, a0, a3)

    total = functools.partial(reduce_pieces, size=dp)
    dec_gu_sum, dec_down_sum = wide(total(dec_gu_grad)), wide(total(dec_down_grad))
    cross = total(jnp.concatenate([cross_output_grad, cross_queries_grad, cross_kv_grad], axis=0))
    enc_gu_sum, enc_down_sum = wide(total(enc_gu_grad)), wide(total(enc_down_grad))
    dec_att = total(jnp.concatenate([dec_out_grad, dec_in_grad], axis=0))
    enc_att = total(jnp.concatenate([enc_out_grad, enc_in_grad], axis=0))
    gains = gains_mid + gains_end
    gains = jnp.concatenate([gains[:5], gain5[:1]], axis=0)
    gains = sum_all(gains, [("tensor", 4)])
    tables = jnp.stack([enc_table[:heads, :BUCKETS], dec_table[:heads, :BUCKETS]])
    small = jnp.concatenate([gains.reshape(-1), tables.reshape(-1)])
    small = sum_all(small, [("dp", dp)])
    gains = small[:gains.size].reshape(gains.shape)
    tables = small[gains.size:].reshape(tables.shape)
    unfold = lambda g, parts: jnp.transpose(wide(g).reshape(parts, inner, width), (2, 0, 1))
    return (
        encoder_result,
        decoder_result,
        encoder_rows_gradient,
        decoder_rows_gradient,
        gains,
        unfold(enc_att[inner:], 3),
        wide(enc_att[:inner]),
        enc_gu_sum.reshape(encoder_gate_up.shape),
        enc_down_sum,
        unfold(dec_att[inner:], 3),
        wide(dec_att[:inner]),
        jnp.transpose(wide(cross[inner:2 * inner])),
        unfold(cross[2 * inner:], 2),
        wide(cross[:inner]),
        dec_gu_sum.reshape(decoder_gate_up.shape),
        dec_down_sum,
        jnp.transpose(tables, (0, 2, 1)),
    )


def solution(mesh):
    return jax.shard_map(
        functools.partial(local, dict(mesh.shape)),
        mesh=mesh,
        in_specs=(
            P(("dp", "tensor"), None),
            P(("dp", "tensor"), None),
            P("dp", None),
            P("dp", None),
            P(),
            P(None, None, "tensor"),
            P("tensor", None),
            P(None, None, "tensor"),
            P("tensor", None),
            P(None, None, "tensor"),
            P("tensor", None),
            P(None, "tensor"),
            P(None, None, "tensor"),
            P("tensor", None),
            P(None, None, "tensor"),
            P("tensor", None),
            P(None, None, "tensor"),
            P(("dp", "tensor"), None),
            P(("dp", "tensor"), None),
        ),
        out_specs=(
            P(("dp", "tensor"), None),
            P(("dp", "tensor"), None),
            P(("dp", "tensor"), None),
            P(("dp", "tensor"), None),
            P(),
            P(None, None, "tensor"),
            P("tensor", None),
            P(None, None, "tensor"),
            P("tensor", None),
            P(None, None, "tensor"),
            P("tensor", None),
            P(None, "tensor"),
            P(None, None, "tensor"),
            P("tensor", None),
            P(None, None, "tensor"),
            P("tensor", None),
            P(None, None, "tensor"),
        ),
        check_vma=False,
    )
```
